32 devices in a mesh: seq: 8 (over y, x, core), chan: 4 (over z).
Axes of the slice: x: 2, y: 2, z: 4, core: 2. Of those that a mesh axis runs over, the one named last changes fastest.
Arguments:
- frames: bfloat16 [10, 1536, 4096], P(None, 'chan', 'seq'), may hold values from -6 to 6
- conv_taps: float32 [4, 1536], P(None, 'chan'), may hold values from -3 to 3
- left_factor: bfloat16 [8, 512, 512], P('seq'), may hold values from -0.25 to 0.25
- right_factor: bfloat16 [512, 8, 8], P('seq'), may hold values from -2 to 2
- out_grad: bfloat16 [10, 1536, 4096], P(None, 'chan', 'seq'), may hold values from -6 to 6
Outputs:
- mixed: bfloat16 [10, 1536, 4096], P(None, 'chan', 'seq')
- frames_grad: bfloat16 [10, 1536, 4096], P(None, 'chan', 'seq')
- left_grad: float32 [8, 512, 512], P('seq', 'chan')
- right_grad: float32 [512, 8, 8], P('seq', 'chan')
The draws below stay inside these ranges and needn't reach their ends.
All inputs are finite; a program needn't handle non-finite values.
Results may differ from the reference program's by a relative error of at most 0.0057.
Values may be sent and summed in bfloat16 or wider, within the bound.
A program may use at most 128 MiB of HBM per device.

```python
from functools import partial
import jax
import jax.numpy as jnp
from jax import lax

D = 1536
BLK = 512
TAPS = 4
CLIPS = 10
NBLK = 8
L = 4096


def steps_of(own_key, shape, split, least, largest):
    def one(axis_at, parts):
        heights = jax.random.uniform(jax.random.fold_in(jax.random.fold_in(own_key, 6), axis_at), (parts,), jnp.float32, least / len(split), largest / len(split))
        return jnp.repeat(jnp.exp(heights), shape[axis_at] // parts).reshape((-1,) + (1,) * (len(shape) - axis_at - 1))

    level = one(*split[0])
    for cut in split[1:]:
        level = level * one(*cut)
    return level


def centred(key, extent, scale, reach, cuts=(), held_as=jnp.bfloat16):
    drawn = scale * jax.random.normal(key, extent, jnp.float32)
    if cuts:
        drawn = drawn * steps_of(key, extent, cuts, -0.22, 0.18)
    return jnp.clip(drawn, -reach, reach).astype(held_as)


def setup_inputs(seed: int = 0) -> dict:
    key_list = jax.random.split(jax.random.key(seed), 6)
    return {
        "frames": centred(key_list[0], (CLIPS, D, L), 1.0, 6.0, ((1, 4), (2, 8))),
        "conv_taps": centred(key_list[1], (TAPS, D), 0.5, 3.0, ((1, 4),), jnp.float32),
        "left_factor": centred(key_list[2], (NBLK, BLK, BLK), BLK ** -0.5, 0.25, ((0, 8),)),
        "right_factor": centred(key_list[3], (BLK, NBLK, NBLK), NBLK ** -0.5, 2.0, ((0, 8),)),
        "out_grad": centred(key_list[4], (CLIPS, D, L), 1.0, 6.0, ((1, 4), (2, 8))),
    }


def clip_pass(left_w, right_w, taps, carry, pair):
    clip, cot = pair
    left_sum, right_sum = carry
    xf = clip.astype(jnp.float32)
    padded = jnp.pad(xf, ((0, 0), (TAPS - 1, 0)))
    mixed_conv = jnp.zeros((D, L), jnp.float32)
    for step in range(TAPS):
        mixed_conv = mixed_conv + taps[step][:, None] * padded[:, TAPS - 1 - step:TAPS - 1 - step + L]
    conv = mixed_conv.astype(jnp.bfloat16)
    blocks = conv.astype(jnp.float32).reshape(D, NBLK, BLK)
    first = jnp.einsum('dij,ijk->dik', blocks, left_w.astype(jnp.float32)).astype(jnp.bfloat16)
    firstf = first.astype(jnp.float32)
    second = jnp.einsum('dik,kim->dkm', firstf, right_w.astype(jnp.float32)).reshape(D, L)
    sig = jax.nn.sigmoid(xf)
    gate = xf * sig
    output = (second * gate).astype(jnp.bfloat16)
    cotf = cot.astype(jnp.float32)
    dsecond = (cotf * gate).astype(jnp.bfloat16)
    gate_part = cotf * second * sig * (1.0 + xf * (1.0 - sig))
    dsb = dsecond.astype(jnp.float32).reshape(D, BLK, NBLK)
    right_part = jnp.einsum('dik,dkm->kim', firstf, dsb)
    dfirst = jnp.einsum('dkm,kim->dik', dsb, right_w.astype(jnp.float32)).astype(jnp.bfloat16)
    dff = dfirst.astype(jnp.float32)
    left_part = jnp.einsum('dij,dik->ijk', blocks, dff)
    dconv = jnp.einsum('dik,ijk->dij', dff, left_w.astype(jnp.float32)).reshape(D, L)
    padded_back = jnp.pad(dconv, ((0, 0), (0, TAPS - 1)))
    conv_back = jnp.zeros((D, L), jnp.float32)
    for step in range(TAPS):
        conv_back = conv_back + taps[step][:, None] * padded_back[:, step:step + L]
    grad_out = (gate_part + conv_back).astype(jnp.bfloat16)
    return (left_sum + left_part, right_sum + right_part), (output, grad_out)


def reference(frames, conv_taps, left_factor, right_factor, out_grad):
    stepper = partial(clip_pass, left_factor, right_factor, conv_taps.astype(jnp.float32))
    start = (jnp.zeros((NBLK, BLK, BLK), jnp.float32), jnp.zeros((BLK, NBLK, NBLK), jnp.float32))
    sums, outs = lax.scan(stepper, start, (frames, out_grad))
    return outs[0], outs[1], sums[0], sums[1]
```

```python
import functools

import jax
import jax.numpy as jnp
from jax import lax
from jax.experimental import pallas as pl
from jax.experimental.pallas import tpu as pltpu
from jax.sharding import PartitionSpec as P

TAPS = 4
LANES = 128
EDGE = 16
BACK = 8
LAG = 4
F32 = jnp.float32
BF16 = jnp.bfloat16
MESH = pl.DeviceIdType.MESH


def dot(a, b, ca, cb):
    return lax.dot_general(a, b, (((ca,), (cb,)), ((), ())), preferred_element_type=F32)


def block_kernel(
    nseq, nchan,
    frames_hbm, grad_hbm, taps_ref, left_ref, right_ref,
    mixed_hbm, fgrad_hbm, lgrad_ref, rgrad_ref,
    fr, og, sa, ra, sb, rb, conv, mix, fg, gp, work, dsec, left_t, wide, acc_r, acc_l,
    tapb, edge, edge_s, edge_r, back_s, back_r, lsend, lrecv, rsend, rrecv,
    in_sem, out_sem, a_send, a_recv, b_send, b_recv, edge_sem, back_send, back_recv, sum_sem,
):
    clips, chans, rows = fr.shape
    keep = rows // nseq
    inner = rows // keep
    part = rows // nchan
    step_rows = 32
    me = lax.axis_index("seq")
    z = lax.axis_index("chan")
    nxt = lax.rem(me + 1, nseq)
    prv = lax.rem(me + nseq - 1, nseq)
    mine = pl.ds(pl.multiple_of(me * keep, keep), keep)

    def load(c, which):
        source, held = ((frames_hbm, fr), (grad_hbm, og))[which]
        return pltpu.make_async_copy(source.at[c], held.at[c], in_sem.at[which, c])

    def store(c, which):
        held, target = ((mix, mixed_hbm), (fg, fgrad_hbm))[which]
        return pltpu.make_async_copy(held.at[c], target.at[c], out_sem.at[which, c])

    def remote(src, dst, send, recv, axis, to):
        return pltpu.make_async_remote_copy(
            src_ref=src, dst_ref=dst, send_sem=send, recv_sem=recv,
            device_id={axis: to}, device_id_type=MESH,
        )

    @pl.loop(0, clips)
    def _(c):
        load(c, 0).start()

    @pl.loop(0, clips)
    def _(c):
        load(c, 1).start()

    barrier = pltpu.get_barrier_semaphore()
    for p in range(1, nseq):
        pl.semaphore_signal(
            barrier, inc=1, device_id={"seq": lax.rem(me + p, nseq)}, device_id_type=MESH
        )
    for p in range(1, nchan):
        pl.semaphore_signal(
            barrier, inc=1, device_id={"chan": lax.rem(z + p, nchan)}, device_id_type=MESH
        )

    pick = (
        lax.broadcasted_iota(jnp.int32, (EDGE, LANES), 1)
        == lax.broadcasted_iota(jnp.int32, (EDGE, LANES), 0) + (LANES - EDGE)
    )
    pick_in = jnp.where(pick, 1.0, 0.0).astype(BF16)

    @pl.loop(0, clips)
    def _(c):
        load(c, 0).wait()
        edge_s[c] = dot(pick_in, fr[c, :, rows - LANES :], 1, 1).astype(BF16)

    pl.semaphore_wait(barrier, nseq + nchan - 2)
    edge_copy = remote(edge_s, edge_r, edge_sem.at[0], edge_sem.at[1], "seq", nxt)
    edge_copy.start()

    left_t[...] = left_ref[...].astype(F32).T.astype(BF16)
    for k in range(TAPS):
        tapb[k] = jnp.broadcast_to(taps_ref[:, k : k + 1], (chans, LANES))
    spread = (
        lax.rem(lax.broadcasted_iota(jnp.int32, (inner, rows), 1), inner)
        == lax.broadcasted_iota(jnp.int32, (inner, rows), 0)
    )
    spread = jnp.where(spread, 1.0, 0.0).astype(BF16)
    own_k = (
        lax.rem(lax.broadcasted_iota(jnp.int32, (rows, rows), 0), keep)
        == lax.broadcasted_iota(jnp.int32, (rows, rows), 1) // inner
    )
    wide[...] = jnp.where(own_k, dot(right_ref[...], spread, 1, 0), 0.0).astype(BF16)
    acc_r[...] = jnp.zeros_like(acc_r)
    acc_l[...] = jnp.zeros_like(acc_l)
    pick_prev = jnp.where(jnp.logical_and(pick, me > 0), 1.0, 0.0).astype(BF16)
    pick_next = (
        lax.broadcasted_iota(jnp.int32, (2 * BACK, LANES), 1)
        == lax.rem(lax.broadcasted_iota(jnp.int32, (2 * BACK, LANES), 0), BACK)
    )
    pick_next = jnp.where(jnp.logical_and(pick_next, me < nseq - 1), 1.0, 0.0).astype(BF16)
    edge_copy.wait()

    def tap(k, at):
        return jnp.concatenate([tapb[k, at, :]] * (rows // LANES), axis=1)

    def chunks(body):
        @pl.loop(0, chans // step_rows)
        def _(r):
            body(pl.ds(pl.multiple_of(r * step_rows, step_rows), step_rows))

    def scatter(c, src, dst, send, recv):
        @pl.loop(1, nseq)
        def _(p):
            to = lax.rem(me + p, nseq)
            there = pl.ds(pl.multiple_of(to * keep, keep), keep)
            remote(src.at[c, there], dst.at[c, mine], send.at[c], recv.at[c], "seq", to).start()

    def arrivals(c, src, dst, send, recv):
        others = pl.ds(0, (nseq - 1) * keep)
        return remote(src.at[c, others], dst.at[c, others], send.at[c], recv.at[c], "seq", nxt)

    @pl.loop(0, clips)
    def _(c):
        edge[...] = dot(edge_r[c], pick_prev, 0, 0)

        def body(at):
            x = jnp.concatenate([edge[at, :], fr[c, at, :].astype(F32)], axis=1)
            total = tap(0, at) * x[:, LANES:]
            for k in range(1, TAPS):
                total = total + tap(k, at) * pltpu.roll(x, k, 1)[:, LANES:]
            conv[c, at, :] = total.astype(BF16)

        chunks(body)
        sa[c] = dot(left_t[...], conv[c], 1, 1).astype(BF16)
        scatter(c, sa, ra, a_send, a_recv)
        ra[c, mine, :] = sa[c, mine, :]

    def forward(c):
        load(c, 1).wait()
        arrivals(c, sa, ra, a_send, a_recv).wait_recv()
        work[...] = dot(ra[c], wide[...], 0, 0)

        def body(at):
            x = fr[c, at, :].astype(F32)
            g = og[c, at, :].astype(F32)
            second = work[at, :]
            sig = jax.nn.sigmoid(x)
            gate = x * sig
            mix[c, at, :] = (second * gate).astype(BF16)
            dsec[at, :] = (g * gate).astype(BF16)
            gp[c, at, :] = g * second * sig * (1.0 + x * (1.0 - sig))

        chunks(body)
        sb[c] = dot(wide[...], dsec[...], 1, 1).astype(BF16)
        scatter(c, sb, rb, b_send, b_recv)
        rb[c, mine, :] = sb[c, mine, :]
        acc_r[...] += dot(ra[c], dsec[...], 1, 0)
        store(c, 0).start()

    def sum_right(p):
        to = lax.rem(z + p, nchan)
        there = pl.ds(pl.multiple_of(to * part, part), part)
        return remote(
            rsend.at[there], rrecv.at[p - 1], sum_sem.at[0, p - 1], sum_sem.at[1, p - 1], "chan", to
        )

    def sum_left(p):
        to = lax.rem(z + p, nchan)
        there = pl.ds(pl.multiple_of(to * part, part), part)
        return remote(
            lsend.at[there], lrecv.at[p - 1], sum_sem.at[2, p - 1], sum_sem.at[3, p - 1], "chan", to
        )

    def send_right():
        own = jnp.where(own_k, acc_r[...], 0.0)
        fold = (
            lax.rem(lax.broadcasted_iota(jnp.int32, (rows, LANES), 0), inner)
            == lax.broadcasted_iota(jnp.int32, (rows, LANES), 1)
        )
        fold = jnp.where(fold, 1.0, 0.0).astype(BF16)
        high = own.astype(BF16)
        rest = own - high.astype(F32)
        mid = rest.astype(BF16)
        low = (rest - mid.astype(F32)).astype(BF16)
        rsend[...] = dot(high, fold, 1, 0) + dot(mid, fold, 1, 0) + dot(low, fold, 1, 0)
        for p in range(1, nchan):
            sum_right(p).start()

    def back_edge(c):
        return remote(back_s.at[c], back_r.at[c], back_send.at[c], back_recv.at[c], "seq", prv)

    def backward(c):
        arrivals(c, sb, rb, b_send, b_recv).wait_recv()
        back_s[c] = dot(left_ref[:EDGE, :], rb[c], 1, 0)[:BACK]
        back_edge(c).start()
        acc_l[...] += dot(rb[c], conv[c], 1, 0)

    def send_left():
        acc_r[...] = acc_l[...].T
        lsend[...] = acc_r[...].astype(BF16)
        for p in range(1, nchan):
            sum_left(p).start()

    def finish(c):
        work[...] = dot(rb[c], left_t[...], 0, 0)
        back_edge(c).wait_recv()
        value = back_r[c]
        high = value.astype(BF16).astype(F32)
        both = jnp.concatenate([high, value - high], axis=0).astype(BF16)
        edge[...] = dot(both, pick_next, 0, 0)

        def body(at):
            d = jnp.concatenate([work[at, :], edge[at, :]], axis=1)
            total = gp[c, at, :] + tap(0, at) * d[:, :rows]
            for k in range(1, TAPS):
                total = total + tap(k, at) * pltpu.roll(d, rows + LANES - k, 1)[:, :rows]
            fg[c, at, :] = total.astype(BF16)

        chunks(body)
        store(c, 1).start()

    @pl.loop(0, clips + LAG + 1)
    def _(t):
        pl.when(t < clips)(lambda: forward(t))
        pl.when(t == clips)(send_right)
        pl.when(jnp.logical_and(t >= LAG, t < clips + LAG))(lambda: backward(t - LAG))
        pl.when(t == clips + LAG - 1)(send_left)
        pl.when(t > LAG)(lambda: finish(t - LAG - 1))

    here = pl.ds(pl.multiple_of(z * part, part), part)
    right_total = rsend[here, :]
    for p in range(1, nchan):
        sum_right(p).wait()
        right_total = right_total + rrecv[p - 1]
    rgrad_ref[...] = right_total
    left_total = acc_r[here, :]
    for p in range(1, nchan):
        sum_left(p).wait()
        left_total = left_total + lrecv[p - 1].astype(F32)
    lgrad_ref[...] = left_total

    @pl.loop(0, clips)
    def _(c):
        arrivals(c, sa, ra, a_send, a_recv).wait_send()
        arrivals(c, sb, rb, b_send, b_recv).wait_send()
        back_edge(c).wait_send()
        store(c, 0).wait()
        store(c, 1).wait()


def shards(nseq, nchan, frames, conv_taps, left_factor, right_factor, out_grad):
    clips, chans, rows = frames.shape
    keep, inner = right_factor.shape[0], right_factor.shape[1]
    part = rows // nchan
    slabs = (clips, rows, chans)
    slots = max(nchan - 1, 1)
    right_rows = jnp.swapaxes(right_factor, 0, 1).reshape(inner * keep, inner)
    vmem = pl.BlockSpec(memory_space=pltpu.VMEM)
    anywhere = pl.BlockSpec(memory_space=pl.ANY)
    dma = pltpu.SemaphoreType.DMA
    mixed, frames_grad, left_grad, right_grad = pl.pallas_call(
        functools.partial(block_kernel, nseq, nchan),
        out_shape=(
            jax.ShapeDtypeStruct(frames.shape, BF16),
            jax.ShapeDtypeStruct(frames.shape, BF16),
            jax.ShapeDtypeStruct((part, rows), F32),
            jax.ShapeDtypeStruct((part, LANES), F32),
        ),
        in_specs=[anywhere, anywhere, vmem, vmem, vmem],
        out_specs=(anywhere, anywhere, vmem, vmem),
        scratch_shapes=[
            pltpu.VMEM(frames.shape, BF16),
            pltpu.VMEM(frames.shape, BF16),
            pltpu.VMEM(slabs, BF16),
            pltpu.VMEM(slabs, BF16),
            pltpu.VMEM(slabs, BF16),
            pltpu.VMEM(slabs, BF16),
            pltpu.VMEM(frames.shape, BF16),
            pltpu.VMEM(frames.shape, BF16),
            pltpu.VMEM(frames.shape, BF16),
            pltpu.VMEM(frames.shape, F32),
            pltpu.VMEM((chans, rows), F32),
            pltpu.VMEM((chans, rows), BF16),
            pltpu.VMEM((rows, rows), BF16),
            pltpu.VMEM((rows, rows), BF16),
            pltpu.VMEM((rows, rows), F32),
            pltpu.VMEM((rows, rows), F32),
            pltpu.VMEM((TAPS, chans, LANES), F32),
            pltpu.VMEM((chans, LANES), F32),
            pltpu.VMEM((clips, EDGE, chans), BF16),
            pltpu.VMEM((clips, EDGE, chans), BF16),
            pltpu.VMEM((clips, BACK, chans), F32),
            pltpu.VMEM((clips, BACK, chans), F32),
            pltpu.VMEM((rows, rows), BF16),
            pltpu.VMEM((slots, part, rows), BF16),
            pltpu.VMEM((rows, LANES), F32),
            pltpu.VMEM((slots, part, LANES), F32),
            dma((2, clips)),
            dma((2, clips)),
            dma((clips,)),
            dma((clips,)),
            dma((clips,)),
            dma((clips,)),
            dma((2,)),
            dma((clips,)),
            dma((clips,)),
            dma((4, slots)),
        ],
        compiler_params=pltpu.CompilerParams(
            collective_id=0, has_side_effects=True, vmem_limit_bytes=60 * 2**20
        ),
    )(frames, out_grad, conv_taps.T, left_factor[0], right_rows)
    right_grad = jnp.swapaxes(right_grad[:, :inner].reshape(-1, keep, inner), 0, 1)
    return mixed, frames_grad, left_grad[None], right_grad


def solution(mesh):
    placed = (
        P(None, "chan", "seq"),
        P(None, "chan"),
        P("seq", None, None),
        P("seq", None, None),
        P(None, "chan", "seq"),
    )
    return jax.shard_map(
        functools.partial(shards, mesh.shape["seq"], mesh.shape["chan"]),
        mesh=mesh,
        in_specs=placed,
        out_specs=(
            P(None, "chan", "seq"),
            P(None, "chan", "seq"),
            P("seq", "chan", None),
            P("seq", "chan", None),
        ),
        check_vma=False,
    )
```

```python
import functools

import jax
import jax.numpy as jnp
from jax import lax
from jax.experimental import pallas as pl
from jax.experimental.pallas import tpu as pltpu
from jax.sharding import PartitionSpec as P

TAPS = 4
LANES = 128
EDGE = 16
BACK = 8
LAG = 4
TAIL = 4
F32 = jnp.float32
BF16 = jnp.bfloat16
MESH = pl.DeviceIdType.MESH


def dot(a, b, ca, cb):
    return lax.dot_general(a, b, (((ca,), (cb,)), ((), ())), preferred_element_type=F32)


def block_kernel(
    nseq, nchan,
    frames_hbm, grad_hbm, taps_ref, left_ref, right_ref,
    mixed_hbm, fgrad_hbm, lgrad_ref, rgrad_ref,
    fr, og, sa, ra, sb, rb, conv, mix, fg, gp, work, dsec, left_t, wide, acc_r, acc_l,
    tapb, edge, edge_s, edge_r, back_s, back_r, lsend, lrecv, rsend, rrecv,
    in_sem, out_sem, a_send, a_recv, b_send, b_recv, edge_sem, back_send, back_recv, sum_sem,
):
    clips, chans, rows = fr.shape
    keep = rows // nseq
    inner = rows // keep
    part = rows // nchan
    step_rows = 32
    me = lax.axis_index("seq")
    z = lax.axis_index("chan")
    nxt = lax.rem(me + 1, nseq)
    prv = lax.rem(me + nseq - 1, nseq)
    mine = pl.ds(pl.multiple_of(me * keep, keep), keep)

    def load(c, which):
        source, held = ((frames_hbm, fr), (grad_hbm, og))[which]
        return pltpu.make_async_copy(source.at[c], held.at[c], in_sem.at[which, c])

    def store(c, which):
        held, target = ((mix, mixed_hbm), (fg, fgrad_hbm))[which]
        return pltpu.make_async_copy(held.at[c], target.at[c], out_sem.at[which, c])

    def remote(src, dst, send, recv, axis, to):
        return pltpu.make_async_remote_copy(
            src_ref=src, dst_ref=dst, send_sem=send, recv_sem=recv,
            device_id={axis: to}, device_id_type=MESH,
        )

    @pl.loop(0, clips)
    def _(c):
        load(c, 0).start()

    @pl.loop(0, clips)
    def _(c):
        load(c, 1).start()

    barrier = pltpu.get_barrier_semaphore()
    for p in range(1, nseq):
        pl.semaphore_signal(
            barrier, inc=1, device_id={"seq": lax.rem(me + p, nseq)}, device_id_type=MESH
        )
    for p in range(1, nchan):
        pl.semaphore_signal(
            barrier, inc=1, device_id={"chan": lax.rem(z + p, nchan)}, device_id_type=MESH
        )

    pick = (
        lax.broadcasted_iota(jnp.int32, (EDGE, LANES), 1)
        == lax.broadcasted_iota(jnp.int32, (EDGE, LANES), 0) + (LANES - EDGE)
    )
    pick_in = jnp.where(pick, 1.0, 0.0).astype(BF16)

    @pl.loop(0, clips)
    def _(c):
        load(c, 0).wait()
        edge_s[c] = dot(pick_in, fr[c, :, rows - LANES :], 1, 1).astype(BF16)

    pl.semaphore_wait(barrier, nseq + nchan - 2)
    edge_copy = remote(edge_s, edge_r, edge_sem.at[0], edge_sem.at[1], "seq", nxt)
    edge_copy.start()

    left_t[...] = left_ref[...].astype(F32).T.astype(BF16)
    for k in range(TAPS):
        tapb[k] = jnp.broadcast_to(taps_ref[k : k + 1, :], (LANES, chans)).T
    pick_prev = jnp.where(jnp.logical_and(pick, me > 0), 1.0, 0.0).astype(BF16)
    pick_next = (
        lax.broadcasted_iota(jnp.int32, (2 * BACK, LANES), 1)
        == lax.rem(lax.broadcasted_iota(jnp.int32, (2 * BACK, LANES), 0), BACK)
    )
    pick_next = jnp.where(jnp.logical_and(pick_next, me < nseq - 1), 1.0, 0.0).astype(BF16)
    edge_copy.wait()

    def tap(k, at):
        return jnp.concatenate([tapb[k, at, :]] * (rows // LANES), axis=1)

    def chunks(body):
        steps = chans // step_rows
        group = max(g for g in (1, 2, 3, 4) if steps % g == 0)

        @pl.loop(0, steps // group)
        def _(r):
            for g in range(group):
                body(pl.ds(pl.multiple_of((r * group + g) * step_rows, step_rows), step_rows))

    def scatter(c, src, dst, send, recv):
        @pl.loop(1, nseq)
        def _(p):
            to = lax.rem(me + p, nseq)
            there = pl.ds(pl.multiple_of(to * keep, keep), keep)
            remote(src.at[c, there], dst.at[c, mine], send.at[c], recv.at[c], "seq", to).start()

    def arrivals(c, src, dst, send, recv):
        others = pl.ds(0, (nseq - 1) * keep)
        return remote(src.at[c, others], dst.at[c, others], send.at[c], recv.at[c], "seq", nxt)

    @pl.loop(0, clips)
    def _(c):
        edge[...] = dot(edge_r[c], pick_prev, 0, 0)

        def body(at):
            x = jnp.concatenate([edge[at, :], fr[c, at, :].astype(F32)], axis=1)
            total = tap(0, at) * x[:, LANES:]
            for k in range(1, TAPS):
                total = total + tap(k, at) * pltpu.roll(x, k, 1)[:, LANES:]
            conv[c, at, :] = total.astype(BF16)

        chunks(body)
        sa[c] = dot(left_t[...], conv[c], 1, 1).astype(BF16)
        scatter(c, sa, ra, a_send, a_recv)
        ra[c, mine, :] = sa[c, mine, :]

    own_k = (
        lax.rem(lax.broadcasted_iota(jnp.int32, (rows, rows), 0), keep)
        == lax.broadcasted_iota(jnp.int32, (rows, rows), 1) // inner
    )
    acc_r[...] = jnp.zeros_like(acc_r)
    acc_l[...] = jnp.zeros_like(acc_l)
    here_k = (
        lax.broadcasted_iota(jnp.int32, (keep, rows), 0)
        == lax.broadcasted_iota(jnp.int32, (keep, rows), 1) // inner
    )
    pair = lax.broadcasted_iota(jnp.int32, (inner * inner, rows), 0)
    column = lax.rem(lax.broadcasted_iota(jnp.int32, (inner * inner, rows), 1), inner)

    @pl.loop(0, inner)
    def _(i):
        choose = jnp.where(pair == column + i * inner, 1.0, 0.0).astype(BF16)
        block = jnp.where(here_k, dot(right_ref[...], choose, 0, 0), 0.0).astype(BF16)
        wide[pl.ds(pl.multiple_of(i * keep, keep), keep), :] = block

    def forward(c):
        load(c, 1).wait()
        arrivals(c, sa, ra, a_send, a_recv).wait_recv()
        work[...] = dot(ra[c], wide[...], 0, 0)

        def body(at):
            x = fr[c, at, :].astype(F32)
            g = og[c, at, :].astype(F32)
            second = work[at, :]
            sig = jax.nn.sigmoid(x)
            gate = x * sig
            mix[c, at, :] = (second * gate).astype(BF16)
            dsec[at, :] = (g * gate).astype(BF16)
            gp[c, at, :] = g * second * sig * (1.0 + x * (1.0 - sig))

        chunks(body)
        sb[c] = dot(wide[...], dsec[...], 1, 1).astype(BF16)
        scatter(c, sb, rb, b_send, b_recv)
        rb[c, mine, :] = sb[c, mine, :]
        acc_r[...] += dot(ra[c], dsec[...], 1, 0)
        store(c, 0).start()

    def sum_right(p):
        to = lax.rem(z + p, nchan)
        there = pl.ds(pl.multiple_of(to * part, part), part)
        return remote(
            rsend.at[there], rrecv.at[p - 1], sum_sem.at[0, p - 1], sum_sem.at[1, p - 1], "chan", to
        )

    def sum_left(p):
        to = lax.rem(z + p, nchan)
        there = pl.ds(pl.multiple_of(to * part, part), part)
        return remote(
            lsend.at[there], lrecv.at[p - 1], sum_sem.at[2, p - 1], sum_sem.at[3, p - 1], "chan", to
        )

    def send_right():
        own = jnp.where(own_k, acc_r[...], 0.0)
        fold = (
            lax.rem(lax.broadcasted_iota(jnp.int32, (rows, LANES), 0), inner)
            == lax.broadcasted_iota(jnp.int32, (rows, LANES), 1)
        )
        fold = jnp.where(fold, 1.0, 0.0).astype(BF16)
        high = own.astype(BF16)
        rest = own - high.astype(F32)
        mid = rest.astype(BF16)
        low = (rest - mid.astype(F32)).astype(BF16)
        rsend[...] = dot(high, fold, 1, 0) + dot(mid, fold, 1, 0) + dot(low, fold, 1, 0)
        for p in range(1, nchan):
            sum_right(p).start()

    def back_edge(c):
        return remote(back_s.at[c], back_r.at[c], back_send.at[c], back_recv.at[c], "seq", prv)

    def backward(c):
        arrivals(c, sb, rb, b_send, b_recv).wait_recv()
        back_s[c] = dot(left_ref[:EDGE, :], rb[c], 1, 0)[:BACK]
        back_edge(c).start()
        acc_l[...] += dot(rb[c], conv[c], 1, 0)

    def send_left():
        acc_r[...] = acc_l[...].T
        lsend[...] = acc_r[...].astype(BF16)
        for p in range(1, nchan):
            sum_left(p).start()

    def finish(c):
        work[...] = dot(rb[c], left_t[...], 0, 0)
        back_edge(c).wait_recv()
        value = back_r[c]
        high = value.astype(BF16).astype(F32)
        both = jnp.concatenate([high, value - high], axis=0).astype(BF16)
        edge[...] = dot(both, pick_next, 0, 0)

        def body(at):
            d = jnp.concatenate([work[at, :], edge[at, :]], axis=1)
            total = gp[c, at, :] + tap(0, at) * d[:, :rows]
            for k in range(1, TAPS):
                total = total + tap(k, at) * pltpu.roll(d, rows + LANES - k, 1)[:, :rows]
            fg[c, at, :] = total.astype(BF16)

        chunks(body)
        store(c, 1).start()

    @pl.loop(0, clips + LAG + TAIL)
    def _(t):
        pl.when(t < clips)(lambda: forward(t))
        pl.when(t == clips)(send_right)
        pl.when(jnp.logical_and(t >= LAG, t < clips + LAG))(lambda: backward(t - LAG))
        pl.when(t == clips + LAG - 1)(send_left)
        pl.when(t >= LAG + TAIL)(lambda: finish(t - LAG - TAIL))

    here = pl.ds(pl.multiple_of(z * part, part), part)
    right_total = rsend[here, :]
    for p in range(1, nchan):
        sum_right(p).wait()
        right_total = right_total + rrecv[p - 1]
    rgrad_ref[...] = right_total
    left_total = acc_r[here, :]
    for p in range(1, nchan):
        sum_left(p).wait()
        left_total = left_total + lrecv[p - 1].astype(F32)
    lgrad_ref[...] = left_total

    @pl.loop(0, clips)
    def _(c):
        arrivals(c, sa, ra, a_send, a_recv).wait_send()
        arrivals(c, sb, rb, b_send, b_recv).wait_send()
        back_edge(c).wait_send()
        store(c, 0).wait()
        store(c, 1).wait()


def shards(nseq, nchan, frames, conv_taps, left_factor, right_factor, out_grad):
    clips, chans, rows = frames.shape
    keep, inner = right_factor.shape[0], right_factor.shape[1]
    part = rows // nchan
    slabs = (clips, rows, chans)
    slots = max(nchan - 1, 1)
    right_rows = jnp.transpose(right_factor, (1, 2, 0)).reshape(inner * inner, keep)
    vmem = pl.BlockSpec(memory_space=pltpu.VMEM)
    anywhere = pl.BlockSpec(memory_space=pl.ANY)
    dma = pltpu.SemaphoreType.DMA
    mixed, frames_grad, left_grad, right_grad = pl.pallas_call(
        functools.partial(block_kernel, nseq, nchan),
        out_shape=(
            jax.ShapeDtypeStruct(frames.shape, BF16),
            jax.ShapeDtypeStruct(frames.shape, BF16),
            jax.ShapeDtypeStruct((part, rows), F32),
            jax.ShapeDtypeStruct((part, LANES), F32),
        ),
        in_specs=[anywhere, anywhere, vmem, vmem, vmem],
        out_specs=(anywhere, anywhere, vmem, vmem),
        scratch_shapes=[
            pltpu.VMEM(frames.shape, BF16),
            pltpu.VMEM(frames.shape, BF16),
            pltpu.VMEM(slabs, BF16),
            pltpu.VMEM(slabs, BF16),
            pltpu.VMEM(slabs, BF16),
            pltpu.VMEM(slabs, BF16),
            pltpu.VMEM(frames.shape, BF16),
            pltpu.VMEM(frames.shape, BF16),
            pltpu.VMEM(frames.shape, BF16),
            pltpu.VMEM(frames.shape, F32),
            pltpu.VMEM((chans, rows), F32),
            pltpu.VMEM((chans, rows), BF16),
            pltpu.VMEM((rows, rows), BF16),
            pltpu.VMEM((rows, rows), BF16),
            pltpu.VMEM((rows, rows), F32),
            pltpu.VMEM((rows, rows), F32),
            pltpu.VMEM((TAPS, chans, LANES), F32),
            pltpu.VMEM((chans, LANES), F32),
            pltpu.VMEM((clips, EDGE, chans), BF16),
            pltpu.VMEM((clips, EDGE, chans), BF16),
            pltpu.VMEM((clips, BACK, chans), F32),
            pltpu.VMEM((clips, BACK, chans), F32),
            pltpu.VMEM((rows, rows), BF16),
            pltpu.VMEM((slots, part, rows), BF16),
            pltpu.VMEM((rows, LANES), F32),
            pltpu.VMEM((slots, part, LANES), F32),
            dma((2, clips)),
            dma((2, clips)),
            dma((clips,)),
            dma((clips,)),
            dma((clips,)),
            dma((clips,)),
            dma((2,)),
            dma((clips,)),
            dma((clips,)),
            dma((4, slots)),
        ],
        compiler_params=pltpu.CompilerParams(
            collective_id=0, has_side_effects=True, vmem_limit_bytes=60 * 2**20
        ),
    )(frames, out_grad, conv_taps, left_factor[0], right_rows)
    right_grad = jnp.swapaxes(right_grad[:, :inner].reshape(-1, keep, inner), 0, 1)
    return mixed, frames_grad, left_grad[None], right_grad


def solution(mesh):
    placed = (
        P(None, "chan", "seq"),
        P(None, "chan"),
        P("seq", None, None),
        P("seq", None, None),
        P(None, "chan", "seq"),
    )
    return jax.shard_map(
        functools.partial(shards, mesh.shape["seq"], mesh.shape["chan"]),
        mesh=mesh,
        in_specs=placed,
        out_specs=(
            P(None, "chan", "seq"),
            P(None, "chan", "seq"),
            P("seq", "chan", None),
            P("seq", "chan", None),
        ),
        check_vma=False,
    )
```
